32 devices in a mesh: layer: 2 (over y), basis: 4 (over z), tok: 4 (over x, core).
Axes of the slice: x: 2, y: 2, z: 4, core: 2. Of those that a mesh axis runs over, the one named last changes fastest.
Arguments:
- activations: bfloat16 [2048, 8192], P(('layer', 'tok'), 'basis'), parts along dimension 0, may hold values from -16 to 16
- gradients: bfloat16 [2048, 8192], P(('layer', 'tok'), 'basis'), parts along dimension 0, may hold values from -16 to 16
- input_basis: bfloat16 [16384, 8192], P(('layer', 'tok'), 'basis'), parts along dimension 0, may hold values from -0.0625 to 0.0625
- output_basis: bfloat16 [16384, 8192], P(('layer', 'tok'), 'basis'), parts along dimension 0, may hold values from -0.0625 to 0.0625
Outputs:
- eigenvalues: float32 [16384, 8192], P(('layer', 'tok'), 'basis'), parts along dimension 0
The draws below stay inside these ranges and needn't reach their ends.
There are 2 independent parts, one for each index of `layer`. The reference program is written for one: setup_inputs(seed, part) draws one part's arguments, and reference() takes and returns one part's arrays. A program takes and returns all parts, laid end to end along the dimension named above; each array names one. Nothing has to cross between parts.
All inputs are finite; a program needn't handle non-finite values.
Results may differ from the reference program's by a relative error of at most 0.00039.
Values may be sent and summed in bfloat16 or wider, within the bound.
A program may use at most 256 MiB of HBM per device.

```python
import jax
import jax.numpy as jnp
from jax import lax

D = 8192
TOK_DEV = 256
TOKENS = 1024


def token_scales(key, lowest, highest):
    uniform_part = jax.random.uniform(key, (TOKENS,), jnp.float32)
    return jnp.exp(jnp.log(lowest) + uniform_part * (jnp.log(highest) - jnp.log(lowest)))


def scaled_values(key, scales):
    values = jax.random.truncated_normal(key, -4.0, 4.0, (TOKENS, D), jnp.float32)
    return (values * scales[:, None]).astype(jnp.bfloat16)


def draw_activations(key, part):
    scales = token_scales(key, 0.32, 3.2)
    key = jax.random.fold_in(key, 11)
    return scaled_values(key, scales)


def draw_gradients(key, part):
    scales = token_scales(key, 0.32, 3.2)
    key = jax.random.fold_in(key, 23)
    jitter = token_scales(jax.random.fold_in(key, 7), 0.8, 1.25)
    return scaled_values(key, jitter / scales)


def block_scale(stream_key, dims, cuts, low, largest):
    gain = 1.0
    for axis_at, parts in cuts:
        heights = jax.random.uniform(jax.random.fold_in(jax.random.fold_in(stream_key, 6), axis_at), (parts,), jnp.float32, low / len(cuts), largest / len(cuts))
        gain = gain * jnp.repeat(jnp.exp(heights), dims[axis_at] // parts).reshape((-1,) + (1,) * (len(dims) - 1 - axis_at))
    return gain


def bell_draw(own_key, dims, spread, reach, split=(), dtype=jnp.bfloat16):
    result = jax.random.normal(own_key, dims, jnp.float32) * spread
    if len(split) > 0:
        result = block_scale(own_key, dims, split, -0.22, 0.18) * result
    return jnp.clip(result, min=-reach, max=reach).astype(dtype)


def setup_inputs(seed: int = 0, part: int = 0) -> dict:
    arg_keys = jax.random.split(jax.random.key(seed), 5)
    part_keys = jax.random.split(jax.random.fold_in(arg_keys[4], part), 5)
    activations = draw_activations(jax.random.fold_in(jax.random.fold_in(arg_keys[4], part), 71), part)
    gradients = draw_gradients(jax.random.fold_in(jax.random.fold_in(arg_keys[4], part), 71), part)
    input_basis = bell_draw(part_keys[2], (D, D), D ** -0.5, 0.0625, ((0, 4), (1, 4)))
    output_basis = bell_draw(part_keys[3], (D, D), D ** -0.5, 0.0625, ((0, 4), (1, 4)))
    return dict(activations=activations, gradients=gradients, input_basis=input_basis, output_basis=output_basis)


def reference(activations, gradients, input_basis, output_basis):
    projected_inputs = jnp.dot(activations, input_basis, preferred_element_type=jnp.float32)
    squared_inputs = (projected_inputs * projected_inputs).astype(jnp.bfloat16)
    projected_grads = jnp.dot(gradients, output_basis, preferred_element_type=jnp.float32)
    squared_grads = (projected_grads * projected_grads).astype(jnp.bfloat16)
    block_count = TOKENS // TOK_DEV
    input_blocks = squared_inputs.reshape(block_count, TOK_DEV, D)
    grad_blocks = squared_grads.reshape(block_count, TOK_DEV, D)

    def add_block(running, pair):
        partial_sum = lax.dot_general(pair[0], pair[1], (((0,), (0,)), ((), ())), preferred_element_type=jnp.float32)
        return running + partial_sum, None

    running, _ = lax.scan(add_block, jnp.zeros((D, D), jnp.float32), (input_blocks, grad_blocks))
    return running / TOKENS
```

```python
import jax
import jax.numpy as jnp
from jax import lax
from jax.sharding import PartitionSpec as P


def all_tokens_of_own_block(block):
    n_tok, n_basis = lax.axis_size("tok"), lax.axis_size("basis")
    if n_tok == n_basis:
        swaps = [(b * n_tok + t, t * n_tok + b) for b in range(n_basis) for t in range(n_tok)]
        swapped = lax.ppermute(block, ("basis", "tok"), swaps)
        return lax.all_gather(swapped, "basis", axis=0, tiled=True)
    full = lax.all_gather(block, "basis", axis=1, tiled=True)
    return lax.all_to_all(full, "tok", split_axis=1, concat_axis=0, tiled=True)


def project(block, basis_block):
    partial = jnp.dot(
        all_tokens_of_own_block(block), basis_block, preferred_element_type=jnp.float32
    )
    return lax.psum_scatter(partial, "tok", scatter_dimension=0, tiled=True)


def on_device(activations, gradients, input_basis, output_basis):
    tok_rows = activations.shape[0]
    projected_in = project(activations, input_basis)
    squared_in = (projected_in * projected_in).astype(jnp.bfloat16)
    projected_out = project(gradients, output_basis)
    squared_out = (projected_out * projected_out).astype(jnp.bfloat16)
    every_in = all_tokens_of_own_block(squared_in)
    every_out = lax.all_gather(squared_out, "tok", axis=0, tiled=True)
    total_tokens = tok_rows * lax.axis_size("tok")
    summed = lax.dot_general(
        every_in, every_out, (((0,), (0,)), ((), ())), preferred_element_type=jnp.float32
    )
    return summed / total_tokens


def solution(mesh):
    spec = P(("layer", "tok"), "basis")
    return jax.shard_map(
        on_device, mesh=mesh, in_specs=(spec,) * 4, out_specs=spec, check_vma=False
    )
```

```python
import jax
import jax.numpy as jnp
from jax import lax
from jax.experimental import pallas as pl
from jax.experimental.pallas import tpu as pltpu
from jax.sharding import PartitionSpec as P


def all_tokens_of_own_block(block):
    n_tok, n_basis = lax.axis_size("tok"), lax.axis_size("basis")
    if n_tok == n_basis:
        swaps = [(b * n_tok + t, t * n_tok + b) for b in range(n_basis) for t in range(n_tok)]
        swapped = lax.ppermute(block, ("basis", "tok"), swaps)
        return lax.all_gather(swapped, "basis", axis=0, tiled=True)
    full = lax.all_gather(block, "basis", axis=1, tiled=True)
    return lax.all_to_all(full, "tok", split_axis=1, concat_axis=0, tiled=True)


def project(block, basis_block):
    partial = jnp.dot(
        all_tokens_of_own_block(block), basis_block, preferred_element_type=jnp.float32
    )
    return lax.psum_scatter(partial, "tok", scatter_dimension=0, tiled=True)


MESH = pl.DeviceIdType.MESH
SUBS = 2


def relay_kernel(
    acts, grads, u_in, u_out, every_in, every_out, line,
    xg, u, p, got_core, got_x, sq,
    u_sem, line_send, line_recv, xg_send, xg_recv,
    core_send, core_recv, x_send, x_recv, out_send, out_recv,
):
    t, z = lax.axis_index("tok"), lax.axis_index("basis")
    n_tok, n_z = lax.axis_size("tok"), lax.axis_size("basis")
    rows, cols = acts.shape
    sub = rows // SUBS
    core, chip = lax.rem(t, 2), lax.div(t, 2)
    core_peer, x_peer = t + 1 - 2 * core, lax.rem(t + 2, n_tok)

    barrier = pltpu.get_barrier_semaphore()
    for k in range(1, n_tok):
        pl.semaphore_signal(
            barrier, inc=1, device_id={"tok": lax.rem(t + k, n_tok)}, device_id_type=MESH
        )

    @pl.when(z > 0)
    def _():
        pl.semaphore_signal(barrier, inc=1, device_id={"basis": z - 1}, device_id_type=MESH)

    @pl.when(z < n_z - 1)
    def _():
        pl.semaphore_signal(barrier, inc=1, device_id={"basis": z + 1}, device_id_type=MESH)

    @pl.when((z > 0) & (z < n_z - 1))
    def _():
        pl.semaphore_wait(barrier, n_tok + 1)

    @pl.when((z == 0) | (z == n_z - 1))
    def _():
        pl.semaphore_wait(barrier, n_tok)

    def part(s):
        return pl.ds(s * sub, sub)

    own = (acts, grads, sq.at[0])

    def landing(a, src, s):
        return every_in.at[src, part(s)] if a == 2 else xg.at[a, src, part(s)]

    def line_copy(a, f, s, way, source):
        return pltpu.make_async_remote_copy(
            src_ref=source, dst_ref=line.at[a, f, part(s)],
            send_sem=line_send.at[a, f, s, way], recv_sem=line_recv.at[a, f, s],
            device_id={"basis": z + 1 if way else z - 1}, device_id_type=MESH,
        )

    def plane_copy(a, f, s, source):
        return pltpu.make_async_remote_copy(
            src_ref=source, dst_ref=landing(a, t, s),
            send_sem=xg_send.at[a, f, s], recv_sem=xg_recv.at[a, t, s],
            device_id={"tok": f}, device_id_type=MESH,
        )

    def to_plane(a, f, s, source):
        @pl.when(t == f)
        def _():
            pltpu.make_async_copy(source, landing(a, t, s), xg_recv.at[a, t, s]).start()

        @pl.when(t != f)
        def _():
            plane_copy(a, f, s, source).start()

    def send_own(a, s):
        source = own[a].at[part(s)]

        @pl.when(z < n_z - 1)
        def _():
            line_copy(a, z, s, 1, source).start()

        @pl.when(z > 0)
        def _():
            line_copy(a, z, s, 0, source).start()

        to_plane(a, z, s, source)

    def relay(a, d):
        for s in range(SUBS):
            @pl.when(z - d >= 0)
            def _():
                f = z - d
                block = line.at[a, f, part(s)]
                line_copy(a, f, s, 1, block).wait_recv()

                @pl.when(z < n_z - 1)
                def _():
                    line_copy(a, f, s, 1, block).start()

                to_plane(a, f, s, block)

            @pl.when(z + d < n_z)
            def _():
                f = z + d
                block = line.at[a, f, part(s)]
                line_copy(a, f, s, 0, block).wait_recv()

                @pl.when(z > 0)
                def _():
                    line_copy(a, f, s, 0, block).start()

                to_plane(a, f, s, block)

    def arrived(a, src):
        for s in range(SUBS):
            pltpu.make_async_copy(
                landing(a, src, s), landing(a, src, s), xg_recv.at[a, src, s]
            ).wait()

    def sent(a):
        for s in range(SUBS):
            for f in range(n_z):
                source = line.at[a, f, part(s)]

                @pl.when((f <= z) & (z < n_z - 1))
                def _():
                    line_copy(a, f, s, 1, source).wait_send()

                @pl.when((f >= z) & (z > 0))
                def _():
                    line_copy(a, f, s, 0, source).wait_send()

                @pl.when(t != f)
                def _():
                    plane_copy(a, f, s, source).wait_send()

    def load_basis(a):
        return pltpu.make_async_copy((u_in, u_out)[a], u, u_sem.at[a])

    def core_copy(a, c, s):
        return pltpu.make_async_remote_copy(
            src_ref=p.at[a, 2 * c + 1 - core, part(s)], dst_ref=got_core.at[a, c, part(s)],
            send_sem=core_send.at[a, c, s], recv_sem=core_recv.at[a, c, s],
            device_id={"tok": core_peer}, device_id_type=MESH,
        )

    def x_copy(a, s):
        return pltpu.make_async_remote_copy(
            src_ref=p.at[a, x_peer, part(s)], dst_ref=got_x.at[a, part(s)],
            send_sem=x_send.at[a, s], recv_sem=x_recv.at[a, s],
            device_id={"tok": x_peer}, device_id_type=MESH,
        )

    step = 32

    def project(a, tb):
        def body(j, _):
            at = pl.ds(pl.multiple_of(j * 512, 512), 512)
            p[a, tb, :, at] = jnp.dot(xg[a, tb], u[:, at], preferred_element_type=jnp.float32)
            return 0

        lax.fori_loop(0, cols // 512, body, 0)

    def add_core(a, c, s):
        core_copy(a, c, s).wait_recv()

        def body(i, _):
            at = pl.ds(pl.multiple_of(s * sub + i * step, step), step)
            p[a, 2 * c + core, at, :] += got_core[a, c, at, :]
            return 0

        lax.fori_loop(0, sub // step, body, 0)

    def partials(a):
        load_basis(a).wait()
        for src in range(n_tok):
            arrived(a, src)
        for c in (1 - chip, chip):
            project(a, 2 * c + 1 - core)
            for s in range(SUBS):
                core_copy(a, c, s).start()
        project(a, x_peer)
        for s in range(SUBS):
            add_core(a, 1 - chip, s)
            x_copy(a, s).start()
        project(a, t)
        if a == 0:
            load_basis(1).start()
        for s in range(SUBS):
            add_core(a, chip, s)

    def square(a, s):
        x_copy(a, s).wait_recv()

        def body(i, _):
            at = pl.ds(pl.multiple_of(s * sub + i * step, step), step)
            total = p[a, t, at, :] + got_x[a, at, :]
            sq[a, at, :] = (total * total).astype(sq.dtype)
            return 0

        lax.fori_loop(0, sub // step, body, 0)

    def out_copy(k, s):
        return pltpu.make_async_remote_copy(
            src_ref=sq.at[1, part(s)], dst_ref=every_out.at[t, part(s)],
            send_sem=out_send.at[k, s], recv_sem=out_recv.at[t, s],
            device_id={"tok": lax.rem(t + k, n_tok)}, device_id_type=MESH,
        )

    def own_out(s):
        return pltpu.make_async_copy(
            sq.at[1, part(s)], every_out.at[t, part(s)], out_send.at[0, s]
        )

    load_basis(0).start()
    for s in range(SUBS):
        send_own(0, s)
    for d in range(1, n_z):
        relay(0, d)
    for s in range(SUBS):
        send_own(1, s)
    partials(0)
    for d in range(1, n_z):
        relay(1, d)
    for s in range(SUBS):
        square(0, s)
        send_own(2, s)
    partials(1)
    for d in range(1, n_z - 1):
        relay(2, d)
    for s in range(SUBS):
        square(1, s)
        for k in (2, 1, 3):
            out_copy(k, s).start()
        own_out(s).start()
    relay(2, n_z - 1)
    for s in range(SUBS):
        own_out(s).wait()
        for k in range(1, n_tok):
            out_copy(k, s).wait_send()
            src = lax.rem(t + k, n_tok)
            dst = every_out.at[src, part(s)]
            pltpu.make_async_copy(dst, dst, out_recv.at[src, s]).wait()
        for a in range(2):
            x_copy(a, s).wait_send()
            for c in (1 - chip, chip):
                core_copy(a, c, s).wait_send()
    for src in range(n_tok):
        arrived(2, src)
    for a in range(3):
        sent(a)


def relayed(activations, gradients, input_basis, output_basis):
    n_tok, n_z = lax.axis_size("tok"), lax.axis_size("basis")
    rows, cols = activations.shape
    every = jax.ShapeDtypeStruct((n_tok, rows, cols), jnp.bfloat16)
    dma = pltpu.SemaphoreType.DMA
    every_in, every_out, _ = pl.pallas_call(
        relay_kernel,
        out_shape=(every, every, jax.ShapeDtypeStruct((3, n_z, rows, cols), jnp.bfloat16)),
        in_specs=[pl.BlockSpec(memory_space=pl.ANY)] * 4,
        out_specs=(pl.BlockSpec(memory_space=pl.ANY),) * 3,
        scratch_shapes=[
            pltpu.VMEM((2, n_tok, rows, cols), jnp.bfloat16),
            pltpu.VMEM(input_basis.shape, jnp.bfloat16),
            pltpu.VMEM((2, n_tok, rows, cols), jnp.float32),
            pltpu.VMEM((2, 2, rows, cols), jnp.float32),
            pltpu.VMEM((2, rows, cols), jnp.float32),
            pltpu.VMEM((2, rows, cols), jnp.bfloat16),
            dma((2,)),
            dma((3, n_z, SUBS, 2)), dma((3, n_z, SUBS)),
            dma((3, n_z, SUBS)), dma((3, n_tok, SUBS)),
            dma((2, 2, SUBS)), dma((2, 2, SUBS)),
            dma((2, SUBS)), dma((2, SUBS)),
            dma((n_tok, SUBS)), dma((n_tok, SUBS)),
        ],
        compiler_params=pltpu.CompilerParams(
            collective_id=0, has_side_effects=True, vmem_limit_bytes=60 * 2**20
        ),
        cost_estimate=pl.CostEstimate(
            flops=4 * n_tok * rows * input_basis.size, bytes_accessed=2**26, transcendentals=0
        ),
    )(activations, gradients, input_basis, output_basis)
    return every_in.reshape(-1, cols), every_out.reshape(-1, cols)


def gathered(activations, gradients, input_basis, output_basis):
    projected_in = project(activations, input_basis)
    squared_in = (projected_in * projected_in).astype(jnp.bfloat16)
    projected_out = project(gradients, output_basis)
    squared_out = (projected_out * projected_out).astype(jnp.bfloat16)
    return all_tokens_of_own_block(squared_in), lax.all_gather(squared_out, "tok", axis=0, tiled=True)


def on_device(activations, gradients, input_basis, output_basis):
    rows, cols = activations.shape
    n_tok, n_z = lax.axis_size("tok"), lax.axis_size("basis")
    small = rows * cols <= 2**19 and rows % 64 == 0 and cols % 512 == 0
    plan = relayed if n_tok == n_z == 4 and small else gathered
    every_in, every_out = plan(activations, gradients, input_basis, output_basis)
    total_tokens = rows * n_tok
    summed = lax.dot_general(
        every_in, every_out, (((0,), (0,)), ((), ())), preferred_element_type=jnp.float32
    )
    return summed / total_tokens


def solution(mesh):
    spec = P(("layer", "tok"), "basis")
    return jax.shard_map(
        on_device, mesh=mesh, in_specs=(spec,) * 4, out_specs=spec, check_vma=False
    )
```

```python
import jax
import jax.numpy as jnp
from jax import lax
from jax.experimental import pallas as pl
from jax.experimental.pallas import tpu as pltpu
from jax.sharding import PartitionSpec as P


def all_tokens_of_own_block(block):
    n_tok, n_basis = lax.axis_size("tok"), lax.axis_size("basis")
    if n_tok == n_basis:
        swaps = [(b * n_tok + t, t * n_tok + b) for b in range(n_basis) for t in range(n_tok)]
        swapped = lax.ppermute(block, ("basis", "tok"), swaps)
        return lax.all_gather(swapped, "basis", axis=0, tiled=True)
    full = lax.all_gather(block, "basis", axis=1, tiled=True)
    return lax.all_to_all(full, "tok", split_axis=1, concat_axis=0, tiled=True)


def project(block, basis_block):
    partial = jnp.dot(
        all_tokens_of_own_block(block), basis_block, preferred_element_type=jnp.float32
    )
    return lax.psum_scatter(partial, "tok", scatter_dimension=0, tiled=True)


MESH = pl.DeviceIdType.MESH
SUBS = 2


def relay_kernel(
    acts, grads, u_in, u_out, every_in, every_out, line,
    xg, u, p, got_core, got_x, sq,
    u_sem, line_send, line_recv, xg_send, xg_recv,
    pair_send, core_send, core_recv, x_send, x_recv, out_send, out_recv,
):
    t, z = lax.axis_index("tok"), lax.axis_index("basis")
    n_tok, n_z = lax.axis_size("tok"), lax.axis_size("basis")
    rows, cols = acts.shape
    sub = rows // SUBS
    core, chip = lax.rem(t, 2), lax.div(t, 2)
    core_peer, x_peer = t + 1 - 2 * core, lax.rem(t + 2, n_tok)

    barrier = pltpu.get_barrier_semaphore()
    for k in range(1, n_tok):
        pl.semaphore_signal(
            barrier, inc=1, device_id={"tok": lax.rem(t + k, n_tok)}, device_id_type=MESH
        )

    @pl.when(z > 0)
    def _():
        pl.semaphore_signal(barrier, inc=1, device_id={"basis": z - 1}, device_id_type=MESH)

    @pl.when(z < n_z - 1)
    def _():
        pl.semaphore_signal(barrier, inc=1, device_id={"basis": z + 1}, device_id_type=MESH)

    @pl.when((z > 0) & (z < n_z - 1))
    def _():
        pl.semaphore_wait(barrier, n_tok + 1)

    @pl.when((z == 0) | (z == n_z - 1))
    def _():
        pl.semaphore_wait(barrier, n_tok)

    def part(s):
        return pl.ds(s * sub, sub)

    own = (acts, grads, sq.at[0])

    def landing(a, src, s):
        return every_in.at[src, part(s)] if a == 2 else xg.at[a, src, part(s)]

    def line_copy(a, f, s, way, source):
        return pltpu.make_async_remote_copy(
            src_ref=source, dst_ref=line.at[a, f, part(s)],
            send_sem=line_send.at[a, f, s, way], recv_sem=line_recv.at[a, f, s],
            device_id={"basis": z + 1 if way else z - 1}, device_id_type=MESH,
        )

    def plane_copy(a, f, s, source):
        return pltpu.make_async_remote_copy(
            src_ref=source, dst_ref=landing(a, t, s),
            send_sem=xg_send.at[a, f, s], recv_sem=xg_recv.at[a, t, s],
            device_id={"tok": f}, device_id_type=MESH,
        )

    def across(f):
        return lax.div(f, 2) != chip

    def same_parity(f):
        return lax.rem(f, 2) == lax.rem(z, 2)

    def hops_up(f, to):
        last = n_z - 1
        return (to <= last) & ~(across(f) & (to == last) & (lax.rem(f, 2) != last % 2))

    def hops_down(f, to):
        return (to >= 0) & ~(across(f) & (to == 0) & (lax.rem(f, 2) != 0))

    def crosses(f):
        return (t != f) & (~across(f) | same_parity(f))

    def to_plane(a, f, s, source):
        @pl.when(t == f)
        def _():
            pltpu.make_async_copy(source, landing(a, t, s), xg_recv.at[a, t, s]).start()

        @pl.when(crosses(f))
        def _():
            plane_copy(a, f, s, source).start()

    def send_own(a, s):
        source = own[a].at[part(s)]

        @pl.when(hops_up(z, z + 1))
        def _():
            line_copy(a, z, s, 1, source).start()

        @pl.when(hops_down(z, z - 1))
        def _():
            line_copy(a, z, s, 0, source).start()

        to_plane(a, z, s, source)

    def relay(a, s):
        for d in range(1, n_z):
            @pl.when((z - d >= 0) & hops_up(z - d, z))
            def _():
                f = z - d
                block = line.at[a, f, part(s)]
                line_copy(a, f, s, 1, block).wait_recv()

                @pl.when(hops_up(f, z + 1))
                def _():
                    line_copy(a, f, s, 1, block).start()

                to_plane(a, f, s, block)

            @pl.when((z + d < n_z) & hops_down(z + d, z))
            def _():
                f = z + d
                block = line.at[a, f, part(s)]
                line_copy(a, f, s, 0, block).wait_recv()

                @pl.when(hops_down(f, z - 1))
                def _():
                    line_copy(a, f, s, 0, block).start()

                to_plane(a, f, s, block)

    def landed(a, src, s):
        pltpu.make_async_copy(
            landing(a, src, s), landing(a, src, s), xg_recv.at[a, src, s]
        ).wait()

    def pair_copy(a, c, s):
        src = 2 * (1 - chip) + c
        return pltpu.make_async_remote_copy(
            src_ref=landing(a, src, s), dst_ref=landing(a, src, s),
            send_sem=pair_send.at[a, c, s], recv_sem=xg_recv.at[a, src, s],
            device_id={"basis": z + 1 - 2 * lax.rem(z, 2)}, device_id_type=MESH,
        )

    def hand_on(a, s):
        @pl.when(same_parity(t))
        def _():
            for c in range(2):
                landed(a, 2 * (1 - chip) + c, s)
                pair_copy(a, c, s).start()

    def arrived(a, s):
        landed(a, t, s)
        landed(a, core_peer, s)

        @pl.when(~same_parity(t))
        def _():
            for c in range(2):
                landed(a, 2 * (1 - chip) + c, s)

    def sent(a):
        for s in range(SUBS):
            for f in range(n_z):
                source = line.at[a, f, part(s)]

                @pl.when((f <= z) & hops_up(f, z + 1))
                def _():
                    line_copy(a, f, s, 1, source).wait_send()

                @pl.when((f >= z) & hops_down(f, z - 1))
                def _():
                    line_copy(a, f, s, 0, source).wait_send()

                @pl.when(crosses(f))
                def _():
                    plane_copy(a, f, s, source).wait_send()

            @pl.when(same_parity(t))
            def _():
                for c in range(2):
                    pair_copy(a, c, s).wait_send()

    def load_basis(a):
        return pltpu.make_async_copy((u_in, u_out)[a], u, u_sem.at[a])

    def core_copy(a, c, s):
        return pltpu.make_async_remote_copy(
            src_ref=p.at[a, 2 * c + 1 - core, part(s)], dst_ref=got_core.at[a, c, part(s)],
            send_sem=core_send.at[a, c, s], recv_sem=core_recv.at[a, c, s],
            device_id={"tok": core_peer}, device_id_type=MESH,
        )

    def x_copy(a, s):
        return pltpu.make_async_remote_copy(
            src_ref=p.at[a, x_peer, part(s)], dst_ref=got_x.at[a, part(s)],
            send_sem=x_send.at[a, s], recv_sem=x_recv.at[a, s],
            device_id={"tok": x_peer}, device_id_type=MESH,
        )

    step = 32

    def project(a, s):
        def body(j, _):
            at = pl.ds(pl.multiple_of(j * 512, 512), 512)
            left = xg[a, :, part(s), :].reshape(n_tok * sub, cols)
            product = jnp.dot(left, u[:, at], preferred_element_type=jnp.float32)
            p[a, :, part(s), at] = product.reshape(n_tok, sub, 512)
            return 0

        lax.fori_loop(0, cols // 512, body, 0)

    def add_core(a, c, s):
        core_copy(a, c, s).wait_recv()

        def body(i, _):
            at = pl.ds(pl.multiple_of(s * sub + i * step, step), step)
            p[a, 2 * c + core, at, :] += got_core[a, c, at, :]
            return 0

        lax.fori_loop(0, sub // step, body, 0)

    def partials(a, s):
        arrived(a, s)
        project(a, s)
        for c in (1 - chip, chip):
            core_copy(a, c, s).start()
        add_core(a, 1 - chip, s)
        x_copy(a, s).start()
        add_core(a, chip, s)

    def square(a, s):
        x_copy(a, s).wait_recv()

        def body(i, _):
            at = pl.ds(pl.multiple_of(s * sub + i * step, step), step)
            total = p[a, t, at, :] + got_x[a, at, :]
            sq[a, at, :] = (total * total).astype(sq.dtype)
            return 0

        lax.fori_loop(0, sub // step, body, 0)

    def out_copy(k, s):
        return pltpu.make_async_remote_copy(
            src_ref=sq.at[1, part(s)], dst_ref=every_out.at[t, part(s)],
            send_sem=out_send.at[k, s], recv_sem=out_recv.at[t, s],
            device_id={"tok": lax.rem(t + k, n_tok)}, device_id_type=MESH,
        )

    def own_out(s):
        return pltpu.make_async_copy(
            sq.at[1, part(s)], every_out.at[t, part(s)], out_send.at[0, s]
        )

    def finish_out(s):
        square(1, s)
        for k in (2, 1, 3):
            out_copy(k, s).start()
        own_out(s).start()

    load_basis(0).start()
    send_own(0, 0)
    relay(0, 0)
    send_own(0, 1)
    hand_on(0, 0)
    load_basis(0).wait()
    partials(0, 0)
    relay(0, 1)
    send_own(1, 0)
    hand_on(0, 1)
    partials(0, 1)
    load_basis(1).start()
    relay(1, 0)
    send_own(1, 1)
    hand_on(1, 0)
    load_basis(1).wait()
    partials(1, 0)
    relay(1, 1)
    square(0, 0)
    send_own(2, 0)
    hand_on(1, 1)
    square(0, 1)
    send_own(2, 1)
    partials(1, 1)
    relay(2, 0)
    hand_on(2, 0)
    finish_out(0)
    relay(2, 1)
    hand_on(2, 1)
    finish_out(1)
    for s in range(SUBS):
        own_out(s).wait()
        for k in range(1, n_tok):
            out_copy(k, s).wait_send()
            src = lax.rem(t + k, n_tok)
            dst = every_out.at[src, part(s)]
            pltpu.make_async_copy(dst, dst, out_recv.at[src, s]).wait()
        for a in range(2):
            x_copy(a, s).wait_send()
            for c in (1 - chip, chip):
                core_copy(a, c, s).wait_send()
        arrived(2, s)
    for a in range(3):
        sent(a)


def relayed(activations, gradients, input_basis, output_basis):
    n_tok, n_z = lax.axis_size("tok"), lax.axis_size("basis")
    rows, cols = activations.shape
    every = jax.ShapeDtypeStruct((n_tok, rows, cols), jnp.bfloat16)
    dma = pltpu.SemaphoreType.DMA
    every_in, every_out, _ = pl.pallas_call(
        relay_kernel,
        out_shape=(every, every, jax.ShapeDtypeStruct((3, n_z, rows, cols), jnp.bfloat16)),
        in_specs=[pl.BlockSpec(memory_space=pl.ANY)] * 4,
        out_specs=(pl.BlockSpec(memory_space=pl.ANY),) * 3,
        scratch_shapes=[
            pltpu.VMEM((2, n_tok, rows, cols), jnp.bfloat16),
            pltpu.VMEM(input_basis.shape, jnp.bfloat16),
            pltpu.VMEM((2, n_tok, rows, cols), jnp.float32),
            pltpu.VMEM((2, 2, rows, cols), jnp.float32),
            pltpu.VMEM((2, rows, cols), jnp.float32),
            pltpu.VMEM((2, rows, cols), jnp.bfloat16),
            dma((2,)),
            dma((3, n_z, SUBS, 2)), dma((3, n_z, SUBS)),
            dma((3, n_z, SUBS)), dma((3, n_tok, SUBS)),
            dma((3, 2, SUBS)), dma((2, 2, SUBS)), dma((2, 2, SUBS)),
            dma((2, SUBS)), dma((2, SUBS)),
            dma((n_tok, SUBS)), dma((n_tok, SUBS)),
        ],
        compiler_params=pltpu.CompilerParams(
            collective_id=0, has_side_effects=True, vmem_limit_bytes=60 * 2**20
        ),
        cost_estimate=pl.CostEstimate(
            flops=4 * n_tok * rows * input_basis.size, bytes_accessed=2**26, transcendentals=0
        ),
    )(activations, gradients, input_basis, output_basis)
    return every_in.reshape(-1, cols), every_out.reshape(-1, cols)


def gathered(activations, gradients, input_basis, output_basis):
    projected_in = project(activations, input_basis)
    squared_in = (projected_in * projected_in).astype(jnp.bfloat16)
    projected_out = project(gradients, output_basis)
    squared_out = (projected_out * projected_out).astype(jnp.bfloat16)
    return all_tokens_of_own_block(squared_in), lax.all_gather(squared_out, "tok", axis=0, tiled=True)


def on_device(activations, gradients, input_basis, output_basis):
    rows, cols = activations.shape
    n_tok, n_z = lax.axis_size("tok"), lax.axis_size("basis")
    small = rows * cols <= 2**19 and rows % 64 == 0 and cols % 512 == 0
    plan = relayed if n_tok == n_z == 4 and small else gathered
    every_in, every_out = plan(activations, gradients, input_basis, output_basis)
    total_tokens = rows * n_tok
    summed = lax.dot_general(
        every_in, every_out, (((0,), (0,)), ((), ())), preferred_element_type=jnp.float32
    )
    return summed / total_tokens


def solution(mesh):
    spec = P(("layer", "tok"), "basis")
    return jax.shard_map(
        on_device, mesh=mesh, in_specs=(spec,) * 4, out_specs=spec, check_vma=False
    )
```

```python
import jax
import jax.numpy as jnp
from jax import lax
from jax.experimental import pallas as pl
from jax.experimental.pallas import tpu as pltpu
from jax.sharding import PartitionSpec as P


def all_tokens_of_own_block(block):
    n_tok, n_basis = lax.axis_size("tok"), lax.axis_size("basis")
    if n_tok == n_basis:
        swaps = [(b * n_tok + t, t * n_tok + b) for b in range(n_basis) for t in range(n_tok)]
        swapped = lax.ppermute(block, ("basis", "tok"), swaps)
        return lax.all_gather(swapped, "basis", axis=0, tiled=True)
    full = lax.all_gather(block, "basis", axis=1, tiled=True)
    return lax.all_to_all(full, "tok", split_axis=1, concat_axis=0, tiled=True)


def project(block, basis_block):
    partial = jnp.dot(
        all_tokens_of_own_block(block), basis_block, preferred_element_type=jnp.float32
    )
    return lax.psum_scatter(partial, "tok", scatter_dimension=0, tiled=True)


MESH = pl.DeviceIdType.MESH
SUBS = 2


def relay_kernel(
    acts, grads, u_in, u_out, every_in, every_out, line,
    xg, u, p, got_core, got_x, sq,
    u_sem, line_send, line_recv, xg_send, xg_recv,
    pair_send, core_send, core_recv, x_send, x_recv, out_send, out_recv,
):
    t, z = lax.axis_index("tok"), lax.axis_index("basis")
    n_tok, n_z = lax.axis_size("tok"), lax.axis_size("basis")
    rows, cols = acts.shape
    sub = rows // SUBS
    core, chip = lax.rem(t, 2), lax.div(t, 2)
    core_peer, x_peer = t + 1 - 2 * core, lax.rem(t + 2, n_tok)

    barrier = pltpu.get_barrier_semaphore()
    for k in range(1, n_tok):
        pl.semaphore_signal(
            barrier, inc=1, device_id={"tok": lax.rem(t + k, n_tok)}, device_id_type=MESH
        )

    @pl.when(z > 0)
    def _():
        pl.semaphore_signal(barrier, inc=1, device_id={"basis": z - 1}, device_id_type=MESH)

    @pl.when(z < n_z - 1)
    def _():
        pl.semaphore_signal(barrier, inc=1, device_id={"basis": z + 1}, device_id_type=MESH)

    @pl.when((z > 0) & (z < n_z - 1))
    def _():
        pl.semaphore_wait(barrier, n_tok + 1)

    @pl.when((z == 0) | (z == n_z - 1))
    def _():
        pl.semaphore_wait(barrier, n_tok)

    def part(s):
        return pl.ds(s * sub, sub)

    own = (acts, grads, sq.at[0])

    def landing(a, src, s):
        return every_in.at[src, part(s)] if a == 2 else xg.at[a, src, part(s)]

    def line_copy(a, f, s, way, source):
        return pltpu.make_async_remote_copy(
            src_ref=source, dst_ref=line.at[a, f, part(s)],
            send_sem=line_send.at[a, f, s, way], recv_sem=line_recv.at[a, f, s],
            device_id={"basis": z + 1 if way else z - 1}, device_id_type=MESH,
        )

    def plane_copy(a, f, s, source):
        return pltpu.make_async_remote_copy(
            src_ref=source, dst_ref=landing(a, t, s),
            send_sem=xg_send.at[a, f, s], recv_sem=xg_recv.at[a, t, s],
            device_id={"tok": f}, device_id_type=MESH,
        )

    def across(f):
        return lax.div(f, 2) != chip

    def same_parity(f):
        return lax.rem(f, 2) == lax.rem(z, 2)

    def hops_up(f, to):
        last = n_z - 1
        return (to <= last) & ~(across(f) & (to == last) & (lax.rem(f, 2) != last % 2))

    def hops_down(f, to):
        return (to >= 0) & ~(across(f) & (to == 0) & (lax.rem(f, 2) != 0))

    def crosses(f):
        return (t != f) & (~across(f) | same_parity(f))

    def to_plane(a, f, s, source):
        @pl.when(t == f)
        def _():
            pltpu.make_async_copy(source, landing(a, t, s), xg_recv.at[a, t, s]).start()

        @pl.when(crosses(f))
        def _():
            plane_copy(a, f, s, source).start()

    def send_own(a, s):
        source = own[a].at[part(s)]

        @pl.when(hops_up(z, z + 1))
        def _():
            line_copy(a, z, s, 1, source).start()

        @pl.when(hops_down(z, z - 1))
        def _():
            line_copy(a, z, s, 0, source).start()

        to_plane(a, z, s, source)

    def relay(a, s, d):
        @pl.when((z - d >= 0) & hops_up(z - d, z))
        def _():
            f = z - d
            block = line.at[a, f, part(s)]
            line_copy(a, f, s, 1, block).wait_recv()

            @pl.when(hops_up(f, z + 1))
            def _():
                line_copy(a, f, s, 1, block).start()

            to_plane(a, f, s, block)

        @pl.when((z + d < n_z) & hops_down(z + d, z))
        def _():
            f = z + d
            block = line.at[a, f, part(s)]
            line_copy(a, f, s, 0, block).wait_recv()

            @pl.when(hops_down(f, z - 1))
            def _():
                line_copy(a, f, s, 0, block).start()

            to_plane(a, f, s, block)

    def landed(a, src, s):
        pltpu.make_async_copy(
            landing(a, src, s), landing(a, src, s), xg_recv.at[a, src, s]
        ).wait()

    def pair_copy(a, c, s):
        src = 2 * (1 - chip) + c
        return pltpu.make_async_remote_copy(
            src_ref=landing(a, src, s), dst_ref=landing(a, src, s),
            send_sem=pair_send.at[a, c, s], recv_sem=xg_recv.at[a, src, s],
            device_id={"basis": z + 1 - 2 * lax.rem(z, 2)}, device_id_type=MESH,
        )

    def hand_on(a, s):
        @pl.when(same_parity(t))
        def _():
            for c in range(2):
                landed(a, 2 * (1 - chip) + c, s)
                pair_copy(a, c, s).start()

    def arrived(a, s):
        landed(a, t, s)
        landed(a, core_peer, s)

        @pl.when(~same_parity(t))
        def _():
            for c in range(2):
                landed(a, 2 * (1 - chip) + c, s)

    def sent(a):
        for s in range(SUBS):
            for f in range(n_z):
                source = line.at[a, f, part(s)]

                @pl.when((f <= z) & hops_up(f, z + 1))
                def _():
                    line_copy(a, f, s, 1, source).wait_send()

                @pl.when((f >= z) & hops_down(f, z - 1))
                def _():
                    line_copy(a, f, s, 0, source).wait_send()

                @pl.when(crosses(f))
                def _():
                    plane_copy(a, f, s, source).wait_send()

            @pl.when(same_parity(t))
            def _():
                for c in range(2):
                    pair_copy(a, c, s).wait_send()

    def load_basis(a):
        return pltpu.make_async_copy((u_in, u_out)[a], u, u_sem.at[a])

    def core_copy(a, c, s):
        return pltpu.make_async_remote_copy(
            src_ref=p.at[a, 2 * c + 1 - core, part(s)], dst_ref=got_core.at[a, c, part(s)],
            send_sem=core_send.at[a, c, s], recv_sem=core_recv.at[a, c, s],
            device_id={"tok": core_peer}, device_id_type=MESH,
        )

    def x_copy(a, s):
        return pltpu.make_async_remote_copy(
            src_ref=p.at[a, x_peer, part(s)], dst_ref=got_x.at[a, part(s)],
            send_sem=x_send.at[a, s], recv_sem=x_recv.at[a, s],
            device_id={"tok": x_peer}, device_id_type=MESH,
        )

    step = 32

    def project(a, s):
        def body(j, _):
            at = pl.ds(pl.multiple_of(j * 512, 512), 512)
            left = xg[a, :, part(s), :].reshape(n_tok * sub, cols)
            product = jnp.dot(left, u[:, at], preferred_element_type=jnp.float32)
            p[a, :, part(s), at] = product.reshape(n_tok, sub, 512)
            return 0

        lax.fori_loop(0, cols // 512, body, 0)

    def add_core(a, c, s):
        core_copy(a, c, s).wait_recv()

        def body(i, _):
            at = pl.ds(pl.multiple_of(s * sub + i * step, step), step)
            p[a, 2 * c + core, at, :] += got_core[a, c, at, :]
            return 0

        lax.fori_loop(0, sub // step, body, 0)

    def start_sums(a, s):
        arrived(a, s)
        project(a, s)
        for c in (1 - chip, chip):
            core_copy(a, c, s).start()

    def finish_sums(a, s):
        add_core(a, 1 - chip, s)
        x_copy(a, s).start()
        add_core(a, chip, s)

    def square(a, s):
        x_copy(a, s).wait_recv()

        def body(i, _):
            at = pl.ds(pl.multiple_of(s * sub + i * step, step), step)
            total = p[a, t, at, :] + got_x[a, at, :]
            sq[a, at, :] = (total * total).astype(sq.dtype)
            return 0

        lax.fori_loop(0, sub // step, body, 0)

    def out_copy(k, s):
        return pltpu.make_async_remote_copy(
            src_ref=sq.at[1, part(s)], dst_ref=every_out.at[t, part(s)],
            send_sem=out_send.at[k, s], recv_sem=out_recv.at[t, s],
            device_id={"tok": lax.rem(t + k, n_tok)}, device_id_type=MESH,
        )

    def own_out(s):
        return pltpu.make_async_copy(
            sq.at[1, part(s)], every_out.at[t, part(s)], out_send.at[0, s]
        )

    def finish_out(s):
        square(1, s)
        for k in (2, 1, 3):
            out_copy(k, s).start()
        own_out(s).start()

    def advance(before, now):
        hand_on(*before)
        relay(*now, 1)
        if now == (0, 1):
            send_own(1, 0)
            load_basis(0).wait()
        elif now == (1, 0):
            send_own(1, 1)
        elif now == (1, 1):
            square(0, 0)
            send_own(2, 0)
            load_basis(1).wait()
        elif now == (2, 0):
            square(0, 1)
            send_own(2, 1)
        relay(*now, 2)
        if before[0] < 2:
            start_sums(*before)
        if before == (0, 1):
            load_basis(1).start()
        relay(*now, 3)
        if before[0] < 2:
            finish_sums(*before)

    load_basis(0).start()
    send_own(0, 0)
    send_own(0, 1)
    for d in range(1, 4):
        relay(0, 0, d)
    advance((0, 0), (0, 1))
    advance((0, 1), (1, 0))
    advance((1, 0), (1, 1))
    advance((1, 1), (2, 0))
    hand_on(2, 0)
    relay(2, 1, 1)
    finish_out(0)
    relay(2, 1, 2)
    finish_out(1)
    relay(2, 1, 3)
    hand_on(2, 1)
    for s in range(SUBS):
        own_out(s).wait()
        for k in range(1, n_tok):
            out_copy(k, s).wait_send()
            src = lax.rem(t + k, n_tok)
            dst = every_out.at[src, part(s)]
            pltpu.make_async_copy(dst, dst, out_recv.at[src, s]).wait()
        for a in range(2):
            x_copy(a, s).wait_send()
            for c in (1 - chip, chip):
                core_copy(a, c, s).wait_send()
        arrived(2, s)
    for a in range(3):
        sent(a)


def relayed(activations, gradients, input_basis, output_basis):
    n_tok, n_z = lax.axis_size("tok"), lax.axis_size("basis")
    rows, cols = activations.shape
    every = jax.ShapeDtypeStruct((n_tok, rows, cols), jnp.bfloat16)
    dma = pltpu.SemaphoreType.DMA
    every_in, every_out, _ = pl.pallas_call(
        relay_kernel,
        out_shape=(every, every, jax.ShapeDtypeStruct((3, n_z, rows, cols), jnp.bfloat16)),
        in_specs=[pl.BlockSpec(memory_space=pl.ANY)] * 4,
        out_specs=(pl.BlockSpec(memory_space=pl.ANY),) * 3,
        scratch_shapes=[
            pltpu.VMEM((2, n_tok, rows, cols), jnp.bfloat16),
            pltpu.VMEM(input_basis.shape, jnp.bfloat16),
            pltpu.VMEM((2, n_tok, rows, cols), jnp.float32),
            pltpu.VMEM((2, 2, rows, cols), jnp.float32),
            pltpu.VMEM((2, rows, cols), jnp.float32),
            pltpu.VMEM((2, rows, cols), jnp.bfloat16),
            dma((2,)),
            dma((3, n_z, SUBS, 2)), dma((3, n_z, SUBS)),
            dma((3, n_z, SUBS)), dma((3, n_tok, SUBS)),
            dma((3, 2, SUBS)), dma((2, 2, SUBS)), dma((2, 2, SUBS)),
            dma((2, SUBS)), dma((2, SUBS)),
            dma((n_tok, SUBS)), dma((n_tok, SUBS)),
        ],
        compiler_params=pltpu.CompilerParams(
            collective_id=0, has_side_effects=True, vmem_limit_bytes=60 * 2**20
        ),
        cost_estimate=pl.CostEstimate(
            flops=4 * n_tok * rows * input_basis.size, bytes_accessed=2**26, transcendentals=0
        ),
    )(activations, gradients, input_basis, output_basis)
    return every_in.reshape(-1, cols), every_out.reshape(-1, cols)


def gathered(activations, gradients, input_basis, output_basis):
    projected_in = project(activations, input_basis)
    squared_in = (projected_in * projected_in).astype(jnp.bfloat16)
    projected_out = project(gradients, output_basis)
    squared_out = (projected_out * projected_out).astype(jnp.bfloat16)
    return all_tokens_of_own_block(squared_in), lax.all_gather(squared_out, "tok", axis=0, tiled=True)


def on_device(activations, gradients, input_basis, output_basis):
    rows, cols = activations.shape
    n_tok, n_z = lax.axis_size("tok"), lax.axis_size("basis")
    small = rows * cols <= 2**19 and rows % 64 == 0 and cols % 512 == 0
    plan = relayed if n_tok == n_z == 4 and small else gathered
    every_in, every_out = plan(activations, gradients, input_basis, output_basis)
    total_tokens = rows * n_tok
    summed = lax.dot_general(
        every_in, every_out, (((0,), (0,)), ((), ())), preferred_element_type=jnp.float32
    )
    return summed / total_tokens


def solution(mesh):
    spec = P(("layer", "tok"), "basis")
    return jax.shard_map(
        on_device, mesh=mesh, in_specs=(spec,) * 4, out_specs=spec, check_vma=False
    )
```

```python
import jax
import jax.numpy as jnp
from jax import lax
from jax.experimental import pallas as pl
from jax.experimental.pallas import tpu as pltpu
from jax.sharding import PartitionSpec as P


def all_tokens_of_own_block(block):
    n_tok, n_basis = lax.axis_size("tok"), lax.axis_size("basis")
    if n_tok == n_basis:
        swaps = [(b * n_tok + t, t * n_tok + b) for b in range(n_basis) for t in range(n_tok)]
        swapped = lax.ppermute(block, ("basis", "tok"), swaps)
        return lax.all_gather(swapped, "basis", axis=0, tiled=True)
    full = lax.all_gather(block, "basis", axis=1, tiled=True)
    return lax.all_to_all(full, "tok", split_axis=1, concat_axis=0, tiled=True)


def project(block, basis_block):
    partial = jnp.dot(
        all_tokens_of_own_block(block), basis_block, preferred_element_type=jnp.float32
    )
    return lax.psum_scatter(partial, "tok", scatter_dimension=0, tiled=True)


MESH = pl.DeviceIdType.MESH
SUBS = 4


def relay_kernel(
    acts, grads, u_in, u_out, every_in, every_out, line,
    xg, u, p, got_core, got_x, sq,
    u_sem, line_send, line_recv, xg_send, xg_recv,
    pair_send, core_send, core_recv, x_send, x_recv, out_send, out_recv,
):
    t, z = lax.axis_index("tok"), lax.axis_index("basis")
    n_tok, n_z = lax.axis_size("tok"), lax.axis_size("basis")
    rows, cols = acts.shape
    sub = rows // SUBS
    core, chip = lax.rem(t, 2), lax.div(t, 2)
    core_peer, x_peer = t + 1 - 2 * core, lax.rem(t + 2, n_tok)

    barrier = pltpu.get_barrier_semaphore()
    for k in range(1, n_tok):
        pl.semaphore_signal(
            barrier, inc=1, device_id={"tok": lax.rem(t + k, n_tok)}, device_id_type=MESH
        )

    @pl.when(z > 0)
    def _():
        pl.semaphore_signal(barrier, inc=1, device_id={"basis": z - 1}, device_id_type=MESH)

    @pl.when(z < n_z - 1)
    def _():
        pl.semaphore_signal(barrier, inc=1, device_id={"basis": z + 1}, device_id_type=MESH)

    @pl.when((z > 0) & (z < n_z - 1))
    def _():
        pl.semaphore_wait(barrier, n_tok + 1)

    @pl.when((z == 0) | (z == n_z - 1))
    def _():
        pl.semaphore_wait(barrier, n_tok)

    def part(s):
        return pl.ds(s * sub, sub)

    own = (acts, grads, sq.at[0])

    def landing(a, src, s):
        return every_in.at[src, part(s)] if a == 2 else xg.at[a, src, part(s)]

    def line_copy(a, f, s, way, source):
        return pltpu.make_async_remote_copy(
            src_ref=source, dst_ref=line.at[a, f, part(s)],
            send_sem=line_send.at[a, f, s, way], recv_sem=line_recv.at[a, f, s],
            device_id={"basis": z + 1 if way else z - 1}, device_id_type=MESH,
        )

    def plane_copy(a, f, s, source):
        return pltpu.make_async_remote_copy(
            src_ref=source, dst_ref=landing(a, t, s),
            send_sem=xg_send.at[a, f, s], recv_sem=xg_recv.at[a, t, s],
            device_id={"tok": f}, device_id_type=MESH,
        )

    def across(f):
        return lax.div(f, 2) != chip

    def same_parity(f):
        return lax.rem(f, 2) == lax.rem(z, 2)

    def hops_up(f, to):
        last = n_z - 1
        return (to <= last) & ~(across(f) & (to == last) & (lax.rem(f, 2) != last % 2))

    def hops_down(f, to):
        return (to >= 0) & ~(across(f) & (to == 0) & (lax.rem(f, 2) != 0))

    def crosses(f):
        return (t != f) & (~across(f) | same_parity(f))

    def to_plane(a, f, s, source):
        @pl.when(t == f)
        def _():
            pltpu.make_async_copy(source, landing(a, t, s), xg_recv.at[a, t, s]).start()

        @pl.when(crosses(f))
        def _():
            plane_copy(a, f, s, source).start()

    def send_own(a, s):
        source = own[a].at[part(s)]

        @pl.when(hops_up(z, z + 1))
        def _():
            line_copy(a, z, s, 1, source).start()

        @pl.when(hops_down(z, z - 1))
        def _():
            line_copy(a, z, s, 0, source).start()

        to_plane(a, z, s, source)

    def relay(a, s, d):
        @pl.when((z - d >= 0) & hops_up(z - d, z))
        def _():
            f = z - d
            block = line.at[a, f, part(s)]
            line_copy(a, f, s, 1, block).wait_recv()

            @pl.when(hops_up(f, z + 1))
            def _():
                line_copy(a, f, s, 1, block).start()

            to_plane(a, f, s, block)

        @pl.when((z + d < n_z) & hops_down(z + d, z))
        def _():
            f = z + d
            block = line.at[a, f, part(s)]
            line_copy(a, f, s, 0, block).wait_recv()

            @pl.when(hops_down(f, z - 1))
            def _():
                line_copy(a, f, s, 0, block).start()

            to_plane(a, f, s, block)

    def landed(a, src, s):
        pltpu.make_async_copy(
            landing(a, src, s), landing(a, src, s), xg_recv.at[a, src, s]
        ).wait()

    def pair_copy(a, c, s):
        src = 2 * (1 - chip) + c
        return pltpu.make_async_remote_copy(
            src_ref=landing(a, src, s), dst_ref=landing(a, src, s),
            send_sem=pair_send.at[a, c, s], recv_sem=xg_recv.at[a, src, s],
            device_id={"basis": z + 1 - 2 * lax.rem(z, 2)}, device_id_type=MESH,
        )

    def hand_on(a, s):
        @pl.when(same_parity(t))
        def _():
            for c in range(2):
                landed(a, 2 * (1 - chip) + c, s)
                pair_copy(a, c, s).start()

    def arrived(a, s):
        landed(a, t, s)
        landed(a, core_peer, s)

        @pl.when(~same_parity(t))
        def _():
            for c in range(2):
                landed(a, 2 * (1 - chip) + c, s)

    def sent(a):
        for s in range(SUBS):
            for f in range(n_z):
                source = line.at[a, f, part(s)]

                @pl.when((f <= z) & hops_up(f, z + 1))
                def _():
                    line_copy(a, f, s, 1, source).wait_send()

                @pl.when((f >= z) & hops_down(f, z - 1))
                def _():
                    line_copy(a, f, s, 0, source).wait_send()

                @pl.when(crosses(f))
                def _():
                    plane_copy(a, f, s, source).wait_send()

            @pl.when(same_parity(t))
            def _():
                for c in range(2):
                    pair_copy(a, c, s).wait_send()

    def load_basis(a):
        return pltpu.make_async_copy((u_in, u_out)[a], u, u_sem.at[a])

    def core_copy(a, c, s):
        return pltpu.make_async_remote_copy(
            src_ref=p.at[a, 2 * c + 1 - core, part(s)], dst_ref=got_core.at[a, c, part(s)],
            send_sem=core_send.at[a, c, s], recv_sem=core_recv.at[a, c, s],
            device_id={"tok": core_peer}, device_id_type=MESH,
        )

    def x_copy(a, s):
        return pltpu.make_async_remote_copy(
            src_ref=p.at[a, x_peer, part(s)], dst_ref=got_x.at[a, part(s)],
            send_sem=x_send.at[a, s], recv_sem=x_recv.at[a, s],
            device_id={"tok": x_peer}, device_id_type=MESH,
        )

    step = 32

    def project(a, s):
        def body(j, _):
            at = pl.ds(pl.multiple_of(j * 512, 512), 512)
            left = xg[a, :, part(s), :].reshape(n_tok * sub, cols)
            product = jnp.dot(left, u[:, at], preferred_element_type=jnp.float32)
            p[a, :, part(s), at] = product.reshape(n_tok, sub, 512)
            return 0

        lax.fori_loop(0, cols // 512, body, 0)

    def add_core(a, c, s):
        core_copy(a, c, s).wait_recv()

        def body(i, _):
            at = pl.ds(pl.multiple_of(s * sub + i * step, step), step)
            p[a, 2 * c + core, at, :] += got_core[a, c, at, :]
            return 0

        lax.fori_loop(0, sub // step, body, 0)

    def start_sums(a, s):
        arrived(a, s)
        project(a, s)
        for c in (1 - chip, chip):
            core_copy(a, c, s).start()

    def finish_sums(a, s):
        add_core(a, 1 - chip, s)
        x_copy(a, s).start()
        add_core(a, chip, s)

    def square(a, s):
        x_copy(a, s).wait_recv()

        def body(i, _):
            at = pl.ds(pl.multiple_of(s * sub + i * step, step), step)
            total = p[a, t, at, :] + got_x[a, at, :]
            sq[a, at, :] = (total * total).astype(sq.dtype)
            return 0

        lax.fori_loop(0, sub // step, body, 0)

    def out_copy(k, s):
        return pltpu.make_async_remote_copy(
            src_ref=sq.at[1, part(s)], dst_ref=every_out.at[t, part(s)],
            send_sem=out_send.at[k, s], recv_sem=out_recv.at[t, s],
            device_id={"tok": lax.rem(t + k, n_tok)}, device_id_type=MESH,
        )

    def own_out(s):
        return pltpu.make_async_copy(
            sq.at[1, part(s)], every_out.at[t, part(s)], out_send.at[0, s]
        )

    def finish_out(s):
        square(1, s)
        for k in (2, 1, 3):
            out_copy(k, s).start()
        own_out(s).start()

    stages = [(a, s) for a in range(3) for s in range(SUBS)]
    load_basis(0).start()
    send_own(*stages[0])
    send_own(*stages[1])
    for d in (1, 2, 3):
        relay(*stages[0], d)
    for i in range(1, len(stages)):
        before, now = stages[i - 1], stages[i]
        hand_on(*before)
        relay(*now, 1)
        if i + 1 < len(stages):
            after = stages[i + 1]
            if after[0] == 2:
                square(0, after[1])
            send_own(*after)
        if now[0] == 2 and now[1] > 0:
            finish_out(now[1] - 1)
        relay(*now, 2)
        if before[0] < 2:
            if before[1] == 0:
                load_basis(before[0]).wait()
            start_sums(*before)
            if before == (0, SUBS - 1):
                load_basis(1).start()
        if i + 1 == len(stages):
            finish_out(now[1])
        relay(*now, 3)
        if before[0] < 2:
            finish_sums(*before)
    hand_on(*stages[-1])
    for s in range(SUBS):
        own_out(s).wait()
        for k in range(1, n_tok):
            out_copy(k, s).wait_send()
            src = lax.rem(t + k, n_tok)
            dst = every_out.at[src, part(s)]
            pltpu.make_async_copy(dst, dst, out_recv.at[src, s]).wait()
        for a in range(2):
            x_copy(a, s).wait_send()
            for c in (1 - chip, chip):
                core_copy(a, c, s).wait_send()
        arrived(2, s)
    for a in range(3):
        sent(a)


def relayed(activations, gradients, input_basis, output_basis):
    n_tok, n_z = lax.axis_size("tok"), lax.axis_size("basis")
    rows, cols = activations.shape
    every = jax.ShapeDtypeStruct((n_tok, rows, cols), jnp.bfloat16)
    dma = pltpu.SemaphoreType.DMA
    every_in, every_out, _ = pl.pallas_call(
        relay_kernel,
        out_shape=(every, every, jax.ShapeDtypeStruct((3, n_z, rows, cols), jnp.bfloat16)),
        in_specs=[pl.BlockSpec(memory_space=pl.ANY)] * 4,
        out_specs=(pl.BlockSpec(memory_space=pl.ANY),) * 3,
        scratch_shapes=[
            pltpu.VMEM((2, n_tok, rows, cols), jnp.bfloat16),
            pltpu.VMEM(input_basis.shape, jnp.bfloat16),
            pltpu.VMEM((2, n_tok, rows, cols), jnp.float32),
            pltpu.VMEM((2, 2, rows, cols), jnp.float32),
            pltpu.VMEM((2, rows, cols), jnp.float32),
            pltpu.VMEM((2, rows, cols), jnp.bfloat16),
            dma((2,)),
            dma((3, n_z, SUBS, 2)), dma((3, n_z, SUBS)),
            dma((3, n_z, SUBS)), dma((3, n_tok, SUBS)),
            dma((3, 2, SUBS)), dma((2, 2, SUBS)), dma((2, 2, SUBS)),
            dma((2, SUBS)), dma((2, SUBS)),
            dma((n_tok, SUBS)), dma((n_tok, SUBS)),
        ],
        compiler_params=pltpu.CompilerParams(
            collective_id=0, has_side_effects=True, vmem_limit_bytes=60 * 2**20
        ),
        cost_estimate=pl.CostEstimate(
            flops=4 * n_tok * rows * input_basis.size, bytes_accessed=2**26, transcendentals=0
        ),
    )(activations, gradients, input_basis, output_basis)
    return every_in.reshape(-1, cols), every_out.reshape(-1, cols)


def gathered(activations, gradients, input_basis, output_basis):
    projected_in = project(activations, input_basis)
    squared_in = (projected_in * projected_in).astype(jnp.bfloat16)
    projected_out = project(gradients, output_basis)
    squared_out = (projected_out * projected_out).astype(jnp.bfloat16)
    return all_tokens_of_own_block(squared_in), lax.all_gather(squared_out, "tok", axis=0, tiled=True)


def on_device(activations, gradients, input_basis, output_basis):
    rows, cols = activations.shape
    n_tok, n_z = lax.axis_size("tok"), lax.axis_size("basis")
    small = rows * cols <= 2**19 and rows % 64 == 0 and cols % 512 == 0
    plan = relayed if n_tok == n_z == 4 and small else gathered
    every_in, every_out = plan(activations, gradients, input_basis, output_basis)
    total_tokens = rows * n_tok
    summed = lax.dot_general(
        every_in, every_out, (((0,), (0,)), ((), ())), preferred_element_type=jnp.float32
    )
    return summed / total_tokens


def solution(mesh):
    spec = P(("layer", "tok"), "basis")
    return jax.shard_map(
        on_device, mesh=mesh, in_specs=(spec,) * 4, out_specs=spec, check_vma=False
    )
```

```python
import jax
import jax.numpy as jnp
from jax import lax
from jax.experimental import pallas as pl
from jax.experimental.pallas import tpu as pltpu
from jax.sharding import PartitionSpec as P


def all_tokens_of_own_block(block):
    n_tok, n_basis = lax.axis_size("tok"), lax.axis_size("basis")
    if n_tok == n_basis:
        swaps = [(b * n_tok + t, t * n_tok + b) for b in range(n_basis) for t in range(n_tok)]
        swapped = lax.ppermute(block, ("basis", "tok"), swaps)
        return lax.all_gather(swapped, "basis", axis=0, tiled=True)
    full = lax.all_gather(block, "basis", axis=1, tiled=True)
    return lax.all_to_all(full, "tok", split_axis=1, concat_axis=0, tiled=True)


def project(block, basis_block):
    partial = jnp.dot(
        all_tokens_of_own_block(block), basis_block, preferred_element_type=jnp.float32
    )
    return lax.psum_scatter(partial, "tok", scatter_dimension=0, tiled=True)


MESH = pl.DeviceIdType.MESH
SUBS = 4


def relay_kernel(
    acts, grads, u_in, u_out, every_in, every_out, line,
    xg, u, p, got_core, got_x, sq,
    u_sem, line_send, line_recv, xg_send, xg_recv,
    pair_send, core_send, core_recv, x_send, x_recv, out_send, out_recv,
):
    t, z = lax.axis_index("tok"), lax.axis_index("basis")
    n_tok, n_z = lax.axis_size("tok"), lax.axis_size("basis")
    rows, cols = acts.shape
    sub = rows // SUBS
    core, chip = lax.rem(t, 2), lax.div(t, 2)
    core_peer, x_peer = t + 1 - 2 * core, lax.rem(t + 2, n_tok)

    barrier = pltpu.get_barrier_semaphore()
    for k in range(1, n_tok):
        pl.semaphore_signal(
            barrier, inc=1, device_id={"tok": lax.rem(t + k, n_tok)}, device_id_type=MESH
        )

    @pl.when(z > 0)
    def _():
        pl.semaphore_signal(barrier, inc=1, device_id={"basis": z - 1}, device_id_type=MESH)

    @pl.when(z < n_z - 1)
    def _():
        pl.semaphore_signal(barrier, inc=1, device_id={"basis": z + 1}, device_id_type=MESH)

    @pl.when((z > 0) & (z < n_z - 1))
    def _():
        pl.semaphore_wait(barrier, n_tok + 1)

    @pl.when((z == 0) | (z == n_z - 1))
    def _():
        pl.semaphore_wait(barrier, n_tok)

    def part(s):
        return pl.ds(s * sub, sub)

    own = (acts, grads, sq.at[0])

    def landing(a, src, s):
        return every_in.at[src, part(s)] if a == 2 else xg.at[a, src, part(s)]

    def line_copy(a, f, s, way, source):
        return pltpu.make_async_remote_copy(
            src_ref=source, dst_ref=line.at[a, f, part(s)],
            send_sem=line_send.at[a, f, s, way], recv_sem=line_recv.at[a, f, s],
            device_id={"basis": z + 1 if way else z - 1}, device_id_type=MESH,
        )

    def plane_copy(a, f, s, source):
        return pltpu.make_async_remote_copy(
            src_ref=source, dst_ref=landing(a, t, s),
            send_sem=xg_send.at[a, f, s], recv_sem=xg_recv.at[a, t, s],
            device_id={"tok": f}, device_id_type=MESH,
        )

    def across(f):
        return lax.div(f, 2) != chip

    def same_parity(f):
        return lax.rem(f, 2) == lax.rem(z, 2)

    def hops_up(f, to):
        last = n_z - 1
        return (to <= last) & ~(across(f) & (to == last) & (lax.rem(f, 2) != last % 2))

    def hops_down(f, to):
        return (to >= 0) & ~(across(f) & (to == 0) & (lax.rem(f, 2) != 0))

    def crosses(f):
        return (t != f) & (~across(f) | same_parity(f))

    def to_plane(a, f, s, source):
        @pl.when(t == f)
        def _():
            pltpu.make_async_copy(source, landing(a, t, s), xg_recv.at[a, t, s]).start()

        @pl.when(crosses(f))
        def _():
            plane_copy(a, f, s, source).start()

    def send_own(a, s):
        source = own[a].at[part(s)]

        @pl.when(hops_up(z, z + 1))
        def _():
            line_copy(a, z, s, 1, source).start()

        @pl.when(hops_down(z, z - 1))
        def _():
            line_copy(a, z, s, 0, source).start()

        to_plane(a, z, s, source)

    def relay(a, s, d):
        @pl.when((z - d >= 0) & hops_up(z - d, z))
        def _():
            f = z - d
            block = line.at[a, f, part(s)]
            line_copy(a, f, s, 1, block).wait_recv()

            @pl.when(hops_up(f, z + 1))
            def _():
                line_copy(a, f, s, 1, block).start()

            to_plane(a, f, s, block)

        @pl.when((z + d < n_z) & hops_down(z + d, z))
        def _():
            f = z + d
            block = line.at[a, f, part(s)]
            line_copy(a, f, s, 0, block).wait_recv()

            @pl.when(hops_down(f, z - 1))
            def _():
                line_copy(a, f, s, 0, block).start()

            to_plane(a, f, s, block)

    def landed(a, src, s):
        pltpu.make_async_copy(
            landing(a, src, s), landing(a, src, s), xg_recv.at[a, src, s]
        ).wait()

    def pair_copy(a, c, s):
        src = 2 * (1 - chip) + c
        return pltpu.make_async_remote_copy(
            src_ref=landing(a, src, s), dst_ref=landing(a, src, s),
            send_sem=pair_send.at[a, c, s], recv_sem=xg_recv.at[a, src, s],
            device_id={"basis": z + 1 - 2 * lax.rem(z, 2)}, device_id_type=MESH,
        )

    def hand_on(a, s):
        @pl.when(same_parity(t))
        def _():
            for c in range(2):
                landed(a, 2 * (1 - chip) + c, s)
                pair_copy(a, c, s).start()

    def arrived(a, s):
        landed(a, t, s)
        landed(a, core_peer, s)

        @pl.when(~same_parity(t))
        def _():
            for c in range(2):
                landed(a, 2 * (1 - chip) + c, s)

    def sent(a):
        for s in range(SUBS):
            for f in range(n_z):
                source = line.at[a, f, part(s)]

                @pl.when((f <= z) & hops_up(f, z + 1))
                def _():
                    line_copy(a, f, s, 1, source).wait_send()

                @pl.when((f >= z) & hops_down(f, z - 1))
                def _():
                    line_copy(a, f, s, 0, source).wait_send()

                @pl.when(crosses(f))
                def _():
                    plane_copy(a, f, s, source).wait_send()

            @pl.when(same_parity(t))
            def _():
                for c in range(2):
                    pair_copy(a, c, s).wait_send()

    def load_basis(a):
        return pltpu.make_async_copy((u_in, u_out)[a], u, u_sem.at[a])

    def core_copy(a, c, s):
        return pltpu.make_async_remote_copy(
            src_ref=p.at[a, 2 * c + 1 - core, part(s)], dst_ref=got_core.at[a, c, part(s)],
            send_sem=core_send.at[a, c, s], recv_sem=core_recv.at[a, c, s],
            device_id={"tok": core_peer}, device_id_type=MESH,
        )

    def x_copy(a, s):
        return pltpu.make_async_remote_copy(
            src_ref=p.at[a, x_peer, part(s)], dst_ref=got_x.at[a, part(s)],
            send_sem=x_send.at[a, s], recv_sem=x_recv.at[a, s],
            device_id={"tok": x_peer}, device_id_type=MESH,
        )

    step = 32

    def project(a, s):
        def body(j, _):
            at = pl.ds(pl.multiple_of(j * 512, 512), 512)
            left = xg[a, :, part(s), :].reshape(n_tok * sub, cols)
            product = jnp.dot(left, u[:, at], preferred_element_type=jnp.float32)
            p[a, :, part(s), at] = product.reshape(n_tok, sub, 512)
            return 0

        lax.fori_loop(0, cols // 512, body, 0)

    def add_core(a, c, s):
        core_copy(a, c, s).wait_recv()

        def body(i, _):
            at = pl.ds(pl.multiple_of(s * sub + i * step, step), step)
            p[a, 2 * c + core, at, :] += got_core[a, c, at, :]
            return 0

        lax.fori_loop(0, sub // step, body, 0)

    def start_sums(a, s):
        arrived(a, s)
        project(a, s)
        for c in (1 - chip, chip):
            core_copy(a, c, s).start()

    def finish_sums(a, s):
        add_core(a, 1 - chip, s)
        x_copy(a, s).start()
        add_core(a, chip, s)

    def square(a, s):
        x_copy(a, s).wait_recv()

        def body(i, _):
            at = pl.ds(pl.multiple_of(s * sub + i * step, step), step)
            total = p[a, t, at, :] + got_x[a, at, :]
            sq[a, at, :] = (total * total).astype(sq.dtype)
            return 0

        lax.fori_loop(0, sub // step, body, 0)

    def out_copy(k, s):
        return pltpu.make_async_remote_copy(
            src_ref=sq.at[1, part(s)], dst_ref=every_out.at[t, part(s)],
            send_sem=out_send.at[k, s], recv_sem=out_recv.at[t, s],
            device_id={"tok": lax.rem(t + k, n_tok)}, device_id_type=MESH,
        )

    def own_out(s):
        return pltpu.make_async_copy(
            sq.at[1, part(s)], every_out.at[t, part(s)], out_send.at[0, s]
        )

    def finish_out(s):
        square(1, s)
        for k in (2, 1, 3):
            out_copy(k, s).start()
        own_out(s).start()

    stages = [(a, s) for a in range(3) for s in range(SUBS)]
    load_basis(0).start()
    send_own(*stages[0])
    send_own(*stages[1])
    for d in (1, 2, 3):
        relay(*stages[0], d)
    for i in range(1, len(stages)):
        before, now = stages[i - 1], stages[i]
        relay(*now, 1)
        hand_on(*before)
        if i + 1 < len(stages):
            after = stages[i + 1]
            if after[0] == 2:
                square(0, after[1])
            send_own(*after)
        if now[0] == 2 and now[1] > 0:
            finish_out(now[1] - 1)
        relay(*now, 2)
        if before[0] < 2:
            if before[1] == 0:
                load_basis(before[0]).wait()
            start_sums(*before)
            if before == (0, SUBS - 1):
                load_basis(1).start()
        if i + 1 == len(stages):
            finish_out(now[1])
        relay(*now, 3)
        if before[0] < 2:
            finish_sums(*before)
    hand_on(*stages[-1])
    for s in range(SUBS):
        own_out(s).wait()
        for k in range(1, n_tok):
            out_copy(k, s).wait_send()
            src = lax.rem(t + k, n_tok)
            dst = every_out.at[src, part(s)]
            pltpu.make_async_copy(dst, dst, out_recv.at[src, s]).wait()
        for a in range(2):
            x_copy(a, s).wait_send()
            for c in (1 - chip, chip):
                core_copy(a, c, s).wait_send()
        arrived(2, s)
    for a in range(3):
        sent(a)


def relayed(activations, gradients, input_basis, output_basis):
    n_tok, n_z = lax.axis_size("tok"), lax.axis_size("basis")
    rows, cols = activations.shape
    every = jax.ShapeDtypeStruct((n_tok, rows, cols), jnp.bfloat16)
    dma = pltpu.SemaphoreType.DMA
    every_in, every_out, _ = pl.pallas_call(
        relay_kernel,
        out_shape=(every, every, jax.ShapeDtypeStruct((3, n_z, rows, cols), jnp.bfloat16)),
        in_specs=[pl.BlockSpec(memory_space=pl.ANY)] * 4,
        out_specs=(pl.BlockSpec(memory_space=pl.ANY),) * 3,
        scratch_shapes=[
            pltpu.VMEM((2, n_tok, rows, cols), jnp.bfloat16),
            pltpu.VMEM(input_basis.shape, jnp.bfloat16),
            pltpu.VMEM((2, n_tok, rows, cols), jnp.float32),
            pltpu.VMEM((2, 2, rows, cols), jnp.float32),
            pltpu.VMEM((2, rows, cols), jnp.float32),
            pltpu.VMEM((2, rows, cols), jnp.bfloat16),
            dma((2,)),
            dma((3, n_z, SUBS, 2)), dma((3, n_z, SUBS)),
            dma((3, n_z, SUBS)), dma((3, n_tok, SUBS)),
            dma((3, 2, SUBS)), dma((2, 2, SUBS)), dma((2, 2, SUBS)),
            dma((2, SUBS)), dma((2, SUBS)),
            dma((n_tok, SUBS)), dma((n_tok, SUBS)),
        ],
        compiler_params=pltpu.CompilerParams(
            collective_id=0, has_side_effects=True, vmem_limit_bytes=60 * 2**20
        ),
        cost_estimate=pl.CostEstimate(
            flops=4 * n_tok * rows * input_basis.size, bytes_accessed=2**26, transcendentals=0
        ),
    )(activations, gradients, input_basis, output_basis)
    return every_in.reshape(-1, cols), every_out.reshape(-1, cols)


def gathered(activations, gradients, input_basis, output_basis):
    projected_in = project(activations, input_basis)
    squared_in = (projected_in * projected_in).astype(jnp.bfloat16)
    projected_out = project(gradients, output_basis)
    squared_out = (projected_out * projected_out).astype(jnp.bfloat16)
    return all_tokens_of_own_block(squared_in), lax.all_gather(squared_out, "tok", axis=0, tiled=True)


def on_device(activations, gradients, input_basis, output_basis):
    rows, cols = activations.shape
    n_tok, n_z = lax.axis_size("tok"), lax.axis_size("basis")
    small = rows * cols <= 2**19 and rows % 64 == 0 and cols % 512 == 0
    plan = relayed if n_tok == n_z == 4 and small else gathered
    every_in, every_out = plan(activations, gradients, input_basis, output_basis)
    total_tokens = rows * n_tok
    summed = lax.dot_general(
        every_in, every_out, (((0,), (0,)), ((), ())), preferred_element_type=jnp.float32
    )
    return summed / total_tokens


def solution(mesh):
    spec = P(("layer", "tok"), "basis")
    return jax.shard_map(
        on_device, mesh=mesh, in_specs=(spec,) * 4, out_specs=spec, check_vma=False
    )
```
